32 devices in a mesh: parts: 2 (over y), track: 4 (over z), tm: 2 (over x), coef: 2 (over core).
Axes of the slice: x: 2, y: 2, z: 4, core: 2. Of those that a mesh axis runs over, the one named last changes fastest.
Arguments:
- sector_ids: int32 [12288], P(('parts', 'track', 'tm')), parts along dimension 0, may hold values from 0 to 63, as said below
- observed: float32 [3, 12288], P(None, ('parts', 'track', 'tm')), parts along dimension 1, may hold values from -6 to 6
- weights: float32 [3, 12288], P(None, ('parts', 'track', 'tm')), parts along dimension 1, may hold values from 0.3 to 3
- coefficients: float32 [2048, 128], P(('parts', 'track')), parts along dimension 0, may hold values from -6 to 6
- tile_index: int32 [128, 12], P(('parts', 'track', 'tm'), 'coef'), parts along dimension 0, may hold values from 0 to 1023, as said below
- tile_count: int32 [128], P(('parts', 'track', 'tm')), parts along dimension 0, may hold values from 3 to 12
- sensitivity: bfloat16 [128, 12, 3, 128, 128], P(('parts', 'track', 'tm'), 'coef'), parts along dimension 0, may hold values from -0.15625 to 0.15625
Outputs:
- gradient: float32 [2048, 128], P(('parts', 'track')), parts along dimension 0
The draws below stay inside these ranges and needn't reach their ends.
There are 2 independent parts, one for each index of `parts`. The reference program is written for one: setup_inputs(seed, part) draws one part's arguments, and reference() takes and returns one part's arrays. A program takes and returns all parts, laid end to end along the dimension named above; each array names one. Nothing has to cross between parts.
Inputs may be any that keep to these rules, and one draw needn't show every extreme that they name: `sector_ids`: the rows of one index of track and tm fall in at most 192 rows into the 8 consecutive sectors of any one index, and some pair reaches 192; the sectors of each index receive exactly 768 rows in all; each sector holds at most 128 rows, and every index holds a sector with exactly 128. `tile_index`: entries at positions from tile_count on are arbitrary blocks and take no part. Block n belongs to track index n // 256. Of the 48 entries held by one index of track, tm and coef (its sectors' rows, its coef share of the columns), live or not, at most 24 name blocks of any one track index, and every such device has a track index named exactly 24 times.
All inputs are finite; a program needn't handle non-finite values.
Results may differ from the reference program's by a relative error of at most 0.0037.
Values may be sent and summed in bfloat16 or wider, within the bound.
A program may use at most 64 MiB of HBM per device.

```python
import math
import jax
import jax.numpy as jnp
from jax import lax

NBLK = 1024
BLOCK = 128
SLOTS = 128
KT = 12
ROWS_SEC = 96
SEC_DEV = 8
S_DEV = 768
NSEC = 64
SAMPLES = 6144
TCAP = 24
N_TRACK = 4
N_TM = 2
N_COEF = 2


def draw_sector_ids(key, part):
    owners = N_TRACK * N_TM
    mean_share = S_DEV // owners
    subkeys = jax.random.split(jax.random.fold_in(key, 11), 6)
    excess = jax.random.randint(subkeys[0], (owners // 2,), 0, mean_share + 1)
    excess = excess.at[0].set(mean_share)
    multiset = jnp.stack([mean_share + excess, mean_share - excess], axis=1).reshape(owners)
    shifts = jax.random.permutation(subkeys[1], owners)
    column = jnp.arange(owners, dtype=jnp.int32)
    counts = multiset[(column[None, :] + shifts[:, None]) % owners]
    cumulative = jnp.cumsum(counts, axis=1)
    position = jnp.arange(S_DEV, dtype=jnp.int32)
    sorted_owner = jnp.sum((cumulative[:, None, :] <= position[None, :, None]).astype(jnp.int32), axis=2)
    row_keys = jax.random.split(subkeys[2], owners)
    orders = jax.vmap(lambda sub: jax.random.permutation(sub, S_DEV))(row_keys)
    owner_of = jnp.take_along_axis(sorted_owner, orders, axis=1)
    onehot = (owner_of[:, :, None] == column[None, None, :]).astype(jnp.int32)
    ranking = jnp.sum((jnp.cumsum(onehot, axis=1) - 1) * onehot, axis=2)
    earlier = jnp.cumsum(counts, axis=0) - counts
    placing = jnp.take_along_axis(earlier, owner_of, axis=1) + ranking
    half_count = SEC_DEV // 2
    spread = jax.random.randint(subkeys[3], (owners, half_count), 0, SLOTS - ROWS_SEC + 1)
    spread = spread.at[:, 0].set(SLOTS - ROWS_SEC)
    sector_sizes = jnp.stack([ROWS_SEC + spread, ROWS_SEC - spread], axis=2).reshape(owners, 2 * half_count)
    leftover = jnp.full((owners, SEC_DEV - 2 * half_count), ROWS_SEC, jnp.int32)
    sector_sizes = jnp.concatenate([sector_sizes.astype(jnp.int32), leftover], axis=1)
    size_keys = jax.random.split(subkeys[4], owners)
    size_orders = jax.vmap(lambda sub: jax.random.permutation(sub, SEC_DEV))(size_keys)
    sector_sizes = jnp.take_along_axis(sector_sizes, size_orders, axis=1)
    sector_ends = jnp.cumsum(sector_sizes, axis=1)
    sorted_sector = jnp.sum((sector_ends[:, None, :] <= position[None, :, None]).astype(jnp.int32), axis=2)
    label_keys = jax.random.split(subkeys[5], owners)
    label_orders = jax.vmap(lambda sub: jax.random.permutation(sub, S_DEV))(label_keys)
    labels = jnp.take_along_axis(sorted_sector, label_orders, axis=1)
    local_sector = labels[owner_of, placing]
    sector_rows = owner_of * SEC_DEV + local_sector
    return sector_rows.reshape(SAMPLES).astype(jnp.int32)


def draw_tile_index(key, part):
    owners = N_TRACK * N_TM
    half_k = KT // N_COEF
    entries = SEC_DEV * half_k
    holders = owners * N_COEF
    per_track = NBLK // N_TRACK
    subkeys = jax.random.split(jax.random.fold_in(key, 23), 4)
    favored = jax.random.randint(subkeys[0], (holders,), 0, N_TRACK)
    offset = jax.random.randint(subkeys[1], (holders,), 0, N_TRACK - 1)
    column = jnp.arange(entries, dtype=jnp.int32)
    others = (favored[:, None] + 1 + (column[None, :] - TCAP + offset[:, None]) % (N_TRACK - 1)) % N_TRACK
    track_of = jnp.where(column[None, :] < TCAP, favored[:, None], others)
    perm_keys = jax.random.split(subkeys[2], holders)
    orders = jax.vmap(lambda sub: jax.random.permutation(sub, entries))(perm_keys)
    track_of = jnp.take_along_axis(track_of, orders, axis=1)
    within = jax.random.randint(subkeys[3], (holders, entries), 0, per_track)
    blocks = track_of * per_track + within
    blocks = blocks.reshape(owners, N_COEF, SEC_DEV, half_k)
    blocks = jnp.transpose(blocks, (0, 2, 1, 3)).reshape(NSEC, KT)
    return blocks.astype(jnp.int32)


def touch_ends(values, key, smallest, high):
    index_at = [jax.random.randint(jax.random.fold_in(key, axis), (), 0, length) for axis, length in enumerate(values.shape)]
    main_axis = values.shape.index(max(values.shape))
    neighbour = index_at[:main_axis] + [(index_at[main_axis] + 1) % values.shape[main_axis]] + index_at[main_axis + 1:]
    return values.at[tuple(index_at)].set(smallest).at[tuple(neighbour)].set(high)


def shard_levels(own_key, dims, pieces, low, high):
    def one(axis_at, shards_of):
        steps = jax.random.uniform(jax.random.fold_in(jax.random.fold_in(own_key, 6), axis_at), (shards_of,), jnp.float32, low / len(pieces), high / len(pieces))
        return jnp.repeat(jnp.exp(steps), dims[axis_at] // shards_of).reshape((-1,) + (1,) * (len(dims) - axis_at - 1))

    factor_of = one(*pieces[0])
    for cut in pieces[1:]:
        factor_of = factor_of * one(*cut)
    return factor_of


def centred(own_key, dims, deviation, reach, pieces=(), kind=jnp.bfloat16):
    level = shard_levels(own_key, dims, pieces, -0.22, 0.18) if pieces else 1.0
    values = jax.random.normal(own_key, dims, jnp.float32) * deviation * level
    return jnp.minimum(jnp.maximum(values, -reach), reach).astype(kind)


def setup_inputs(seed: int = 0, part: int = 0) -> dict:
    splits = jax.random.split(jax.random.key(seed), 8)
    part_splits = jax.random.split(jax.random.fold_in(splits[7], part), 8)
    sector_ids = draw_sector_ids(jax.random.fold_in(jax.random.fold_in(splits[7], part), 71), part)
    observed = centred(part_splits[1], (3, SAMPLES), 1.0, 6.0, ((1, 8),), jnp.float32)
    weights = jnp.clip(jnp.exp(math.log(3.0) - 2.3025851 * jax.random.uniform(part_splits[2], (3, SAMPLES), jnp.float32) ** shard_levels(part_splits[2], (3, SAMPLES), ((1, 8),), -0.2, 0.2)), 0.3, 3.0)
    coefficients = centred(part_splits[3], (NBLK, BLOCK), 1.0, 6.0, ((0, 4),), jnp.float32)
    tile_index = draw_tile_index(jax.random.fold_in(jax.random.fold_in(splits[7], part), 71), part)
    tile_count = touch_ends(jax.random.randint(part_splits[5], (NSEC,), KT // 4, KT + 1), jax.random.fold_in(part_splits[5], 1), KT // 4, KT).astype(jnp.int32)
    sensitivity = centred(part_splits[6], (NSEC, KT, 3, SLOTS, BLOCK), (KT * BLOCK) ** -0.5, 0.15625, ((0, 8), (1, 2)))
    return {"sector_ids": sector_ids, "observed": observed, "weights": weights, "coefficients": coefficients, "tile_index": tile_index, "tile_count": tile_count, "sensitivity": sensitivity}


HUBER = 2.0

def sector_gradient(bundle):
    tiles_in, blocks, active, observed_tile, weight_tile = bundle
    tiles_wide = tiles_in.astype(jnp.float32)
    blocks = jnp.where(active[:, None], blocks, jnp.zeros_like(blocks))
    predicted = jnp.einsum('kcjb,kb->cj', tiles_wide, blocks.astype(jnp.float32))
    scaled = weight_tile * (predicted - observed_tile)
    force = (weight_tile * scaled / jnp.sqrt(1.0 + (scaled / HUBER) ** 2)).astype(jnp.bfloat16)
    tile_grad = jnp.einsum('kcjb,cj->kb', tiles_wide, force.astype(jnp.float32))
    return jnp.where(active[:, None], tile_grad, jnp.zeros_like(tile_grad))

def reference(sector_ids, observed, weights, coefficients, tile_index, tile_count, sensitivity):
    row_total = sector_ids.shape[0]
    ordering = jnp.argsort(sector_ids, stable=True)
    ranked = sector_ids[ordering]
    starts = jnp.searchsorted(ranked, jnp.arange(NSEC, dtype=jnp.int32)).astype(jnp.int32)
    rank_sorted = jnp.arange(row_total, dtype=jnp.int32) - starts[ranked]
    slot_of = jnp.zeros((row_total,), jnp.int32).at[ordering].set(rank_sorted)
    placing = sector_ids * SLOTS + slot_of
    payload = jnp.concatenate([observed, weights], axis=0)
    packed = jnp.zeros((6, NSEC * SLOTS), jnp.float32).at[:, placing].set(payload)
    packed = jnp.transpose(packed.reshape(6, NSEC, SLOTS), (1, 0, 2))
    observed_tiles = packed[:, :3]
    weight_tiles = packed[:, 3:]
    rounded = coefficients.astype(jnp.bfloat16)
    blocks = rounded[tile_index]
    active = jnp.arange(KT, dtype=jnp.int32)[None, :] < tile_count[:, None]
    tile_grad = lax.map(sector_gradient, (sensitivity, blocks, active, observed_tiles, weight_tiles))
    gradient = jnp.zeros((NBLK, BLOCK), jnp.float32).at[tile_index.reshape(-1)].add(tile_grad.reshape(-1, BLOCK))
    return gradient
```

```python
import functools

import jax
import jax.numpy as jnp
from jax import lax
from jax.experimental import pallas as pl
from jax.experimental.pallas import tpu as pltpu
from jax.sharding import PartitionSpec as P

HUBER = 2.0
F32 = jnp.float32
BF16 = jnp.bfloat16
NT = (((1,), (1,)), ((), ()))
NN = (((1,), (0,)), ((), ()))


def dot(a, b, dims=NN):
    return lax.dot_general(a, b, dims, preferred_element_type=F32)


def iota(shape, dim):
    return lax.broadcasted_iota(jnp.int32, shape, dim)


def kernel(
    dims, count_ref, sid_ref, obs_ref, wts_ref, coef_ref, tile_ref, sens_hbm, out_ref,
    sens, coefs, rows, preds, gsend, grecv,
    sens_sem, coef_send, coef_recv, row_send, row_recv, pred_send, pred_recv, grad_send, grad_recv,
):
    nt, nm, nc, ns, hk, lr = dims
    owners, total = nt * nm, nt * nm * nc
    slots = 128
    per = coef_ref.shape[0]
    nq = sid_ref.shape[0]
    entries = ns * hk
    t, m, c = lax.axis_index("track"), lax.axis_index("tm"), lax.axis_index("coef")
    own = t * nm + m
    me = own * nc + c

    def place(d):
        return {"track": d // (nm * nc), "tm": (d // nc) % nm, "coef": d % nc}

    sector_rows = hk * 3 * slots
    loads = [
        pltpu.make_async_copy(
            sens_hbm.at[pl.ds(s * sector_rows, sector_rows)],
            sens.at[pl.ds(s * sector_rows, sector_rows)],
            sens_sem.at[s],
        )
        for s in range(ns)
    ]
    barrier = pltpu.get_barrier_semaphore()

    @pl.loop(1, total)
    def _(p):
        pl.semaphore_signal(
            barrier, inc=1, device_id=place((me + p) % total), device_id_type=pl.DeviceIdType.MESH
        )

    for load in loads:
        load.start()
    coefs[pl.ds(pl.multiple_of(t * per, per), per)] = coef_ref[...].astype(BF16)
    for q in range(nq):
        lanes = pl.ds(q * 128, 128)
        rows[own, pl.ds(q * 8, 3)] = obs_ref[:, lanes]
        rows[own, pl.ds(q * 8 + 3, 3)] = wts_ref[:, lanes]
        rows[own, pl.ds(q * 8 + 6, 1)] = sid_ref[pl.ds(q, 1), :].astype(F32)
        rows[own, pl.ds(q * 8 + 7, 1)] = jnp.zeros((1, 128), F32)
    pl.semaphore_wait(barrier, total - 1)

    def coef_copy(p, source):
        other = (t + p) % nt
        at = coefs.at[pl.ds(pl.multiple_of(source * per, per), per)]
        return pltpu.make_async_remote_copy(
            src_ref=at, dst_ref=at, send_sem=coef_send.at[p], recv_sem=coef_recv.at[source],
            device_id={"track": other, "tm": m, "coef": c}, device_id_type=pl.DeviceIdType.MESH,
        )

    def row_copy(p, source):
        other = (own + p) % owners
        return pltpu.make_async_remote_copy(
            src_ref=rows.at[source], dst_ref=rows.at[source],
            send_sem=row_send.at[p], recv_sem=row_recv.at[source],
            device_id={"track": other // nm, "tm": other % nm, "coef": c},
            device_id_type=pl.DeviceIdType.MESH,
        )

    def pred_copy(p, source):
        return pltpu.make_async_remote_copy(
            src_ref=preds.at[source], dst_ref=preds.at[source],
            send_sem=pred_send.at[p], recv_sem=pred_recv.at[source],
            device_id={"track": t, "tm": m, "coef": (c + p) % nc},
            device_id_type=pl.DeviceIdType.MESH,
        )

    def grad_copy(p, source):
        other = (me + p) % total
        first = pl.multiple_of((other // (nm * nc)) * lr, lr)
        return pltpu.make_async_remote_copy(
            src_ref=gsend.at[pl.ds(first, lr)], dst_ref=grecv.at[source],
            send_sem=grad_send.at[p], recv_sem=grad_recv.at[source],
            device_id=place(other), device_id_type=pl.DeviceIdType.MESH,
        )

    @pl.loop(1, nt)
    def _(p):
        coef_copy(p, t).start()

    @pl.loop(1, owners)
    def _(p):
        row_copy(p, own).start()

    index = jnp.concatenate([tile_ref[:, pl.ds(k, 1)] for k in range(hk)], axis=0)
    sub = iota((ns, 1), 0)
    count = jnp.zeros((ns, 1), jnp.int32)
    for s in range(ns):
        count = jnp.where(sub == s, count_ref[s], count)
    active = jnp.concatenate(
        [jnp.where(c * hk + k < count, 1.0, 0.0) for k in range(hk)], axis=0
    )
    pick = jnp.where((iota((entries, nt * per), 1) == index) & (active > 0.5), 1.0, 0.0).astype(BF16)
    lane = iota((entries, 128), 1)
    named = (index >= lane * per) & (index < (lane + 1) * per)
    named_f = jnp.where(named, 1.0, 0.0)
    before = jnp.where(iota((entries, entries), 1) < iota((entries, entries), 0), 1.0, 0.0)
    rank = jnp.sum(dot(before.astype(BF16), named_f.astype(BF16)) * named_f, axis=1, keepdims=True)
    track = jnp.sum(jnp.where(named, lane, 0).astype(F32), axis=1, keepdims=True)
    within = index.astype(F32) - track * per + 1.0
    lane_f = lane.astype(F32)
    shift = (lax.rem(me, 128 // lr) * lr).astype(F32)
    marks = []
    for u in range(nt):
        marks.append(
            jnp.sum(
                jnp.where((track == u) & (rank + shift == lane_f), within, 0.0), axis=0, keepdims=True
            )
        )
    wide = iota((entries, nt * lr), 1).astype(F32)
    squeeze = jnp.where(track * lr + rank == wide, 1.0, 0.0).T.astype(BF16)

    @pl.loop(1, nt)
    def _(p):
        coef_copy(nt - p, (t + p) % nt).wait_recv()

    blocks = dot(pick, coefs[...])
    wide_blocks = jnp.concatenate(
        [blocks[k * ns:(k + 1) * ns] for k in range(hk)], axis=1
    ).astype(BF16)
    pixels = 3 * slots

    def tile(s, k):
        return sens[pl.ds((s * hk + k) * pixels, pixels), :]

    which = iota((ns, pixels), 0)
    pred = jnp.zeros((ns, pixels), F32)
    for s in range(ns):
        loads[s].wait()
        part = dot(wide_blocks, jnp.concatenate([tile(s, k) for k in range(hk)], axis=1), NT)
        pred = jnp.where(which == s, part, pred)
    preds[c] = pred

    @pl.loop(1, nc)
    def _(p):
        pred_copy(p, c).start()

    @pl.loop(1, owners)
    def _(p):
        row_copy(owners - p, (own + p) % owners).wait_recv()

    ri, rj = iota((128, 256), 0), iota((128, 256), 1)
    tri = jnp.where((ri < rj) | (rj >= 128), 1.0, 0.0).astype(BF16)
    sector = (own * ns + iota((ns, 128), 0)).astype(F32)
    slot_at = iota((slots, 128), 0).astype(F32)

    def source_rows(o, carry):
        base, grid = carry
        got = rows[o]
        hits = []
        for q in range(nq):
            hits.append(jnp.where(got[q * 8 + 6:q * 8 + 7] == sector, 1.0, 0.0))
        ahead = dot(jnp.concatenate(hits, axis=0).astype(BF16), tri)
        put, high, low = [], [], []
        for q in range(nq):
            hit = hits[q]
            rank_q = ahead[q * ns:(q + 1) * ns, :128] + base
            base = base + ahead[q * ns:(q + 1) * ns, 128:]
            slot = jnp.sum(hit * rank_q, axis=0, keepdims=True)
            put.append(jnp.where(slot == slot_at, 1.0, 0.0).astype(BF16))
            chunk = jnp.concatenate(
                [hit * got[q * 8 + i:q * 8 + i + 1] for i in range(6)], axis=0
            )
            upper = chunk.astype(BF16)
            high.append(upper)
            low.append((chunk - upper.astype(F32)).astype(BF16))
        put = jnp.concatenate(put, axis=1)
        both = jnp.concatenate(
            [jnp.concatenate(high, axis=1), jnp.concatenate(low, axis=1)], axis=0
        )
        return base, grid + dot(both, put, NT)

    _, grid = lax.fori_loop(
        0, owners, source_rows,
        (jnp.zeros((ns, 128), F32), jnp.zeros((12 * ns, slots), F32)),
    )
    grid = grid[:6 * ns] + grid[6 * ns:]

    @pl.loop(1, nc)
    def _(p):
        pred_copy(nc - p, (c + p) % nc).wait_recv()

    pred = preds[0]
    for i in range(1, nc):
        pred = pred + preds[i]
    forces = []
    for i in range(3):
        w = grid[(3 + i) * ns:(4 + i) * ns]
        scaled = w * (pred[:, i * slots:(i + 1) * slots] - grid[i * ns:(i + 1) * ns])
        forces.append(w * scaled * lax.rsqrt(1.0 + (scaled / HUBER) ** 2))
    force = jnp.concatenate(forces, axis=1).astype(BF16)
    which = iota((ns, hk * 128), 0)
    grad = jnp.zeros((ns, hk * 128), F32)
    for s in range(ns):
        part = dot(force, jnp.concatenate([tile(s, k) for k in range(hk)], axis=1))
        grad = jnp.where(which == s, part, grad)
    grad = jnp.concatenate([grad[:, k * 128:(k + 1) * 128] for k in range(hk)], axis=0)
    grad = jnp.where(active > 0.5, grad, 0.0).astype(BF16)
    packed = dot(squeeze, grad)
    line = iota((nt * lr, 128), 0)
    for u in range(nt):
        packed = jnp.where(line == u * lr + lr - 1, marks[u], packed)
    gsend[...] = packed.astype(BF16)
    grecv[me] = gsend[pl.ds(pl.multiple_of(t * lr, lr), lr)]

    @pl.loop(1, total)
    def _(p):
        grad_copy(p, me).start()

    @pl.loop(1, total)
    def _(p):
        grad_copy(total - p, (me + p) % total).wait_recv()

    together = 128 // lr
    at = iota((per, 128), 0).astype(F32) + 1.0

    def gather_group(g, acc):
        base = g * together
        mark = jnp.zeros((1, 128), F32)
        for i in range(together):
            mark = mark + grecv[base + i].astype(F32)[lr - 1:lr]
        terms = jnp.concatenate([grecv[base + i] for i in range(together)], axis=0)
        return acc + dot(jnp.where(at == mark, 1.0, 0.0).astype(BF16), terms)

    out_ref[...] = lax.fori_loop(0, total // together, gather_group, jnp.zeros((per, 128), F32))

    @pl.loop(1, nt)
    def _(p):
        coef_copy(p, t).wait_send()

    @pl.loop(1, owners)
    def _(p):
        row_copy(p, own).wait_send()

    @pl.loop(1, nc)
    def _(p):
        pred_copy(p, c).wait_send()

    @pl.loop(1, total)
    def _(p):
        grad_copy(p, me).wait_send()


def per_device(sector_ids, observed, weights, coefficients, tile_index, tile_count, sensitivity):
    nt, nm, nc = lax.axis_size("track"), lax.axis_size("tm"), lax.axis_size("coef")
    ns, hk = tile_index.shape
    per, width = coefficients.shape
    nq = sector_ids.shape[0] // 128
    slots = sensitivity.shape[3]
    owners, total = nt * nm, nt * nm * nc
    cap = 2 * ns * hk // nt
    lr = (cap + 1 + 15) // 16 * 16
    flat = ns * hk * 3 * slots
    vmem = pl.BlockSpec(memory_space=pltpu.VMEM)
    dma = pltpu.SemaphoreType.DMA
    return pl.pallas_call(
        functools.partial(kernel, (nt, nm, nc, ns, hk, lr)),
        out_shape=jax.ShapeDtypeStruct((per, width), F32),
        in_specs=[pl.BlockSpec(memory_space=pltpu.SMEM)] + [vmem] * 5
        + [pl.BlockSpec(memory_space=pl.ANY)],
        out_specs=vmem,
        scratch_shapes=[
            pltpu.VMEM((flat, width), BF16),
            pltpu.VMEM((nt * per, width), BF16),
            pltpu.VMEM((owners, nq * 8, 128), F32),
            pltpu.VMEM((nc, ns, 3 * slots), F32),
            pltpu.VMEM((nt * lr, width), BF16),
            pltpu.VMEM((total, lr, width), BF16),
            dma((ns,)),
            dma((nt,)), dma((nt,)),
            dma((owners,)), dma((owners,)),
            dma((nc,)), dma((nc,)),
            dma((total,)), dma((total,)),
        ],
        compiler_params=pltpu.CompilerParams(
            collective_id=0, has_side_effects=True, vmem_limit_bytes=40 * 1024 * 1024
        ),
    )(
        tile_count,
        sector_ids.reshape(nq, 128),
        observed,
        weights,
        coefficients,
        tile_index,
        sensitivity.reshape(flat, width),
    )


def solution(mesh):
    placed = (
        P(("parts", "track", "tm")),
        P(None, ("parts", "track", "tm")),
        P(None, ("parts", "track", "tm")),
        P(("parts", "track"), None),
        P(("parts", "track", "tm"), "coef"),
        P(("parts", "track", "tm")),
        P(("parts", "track", "tm"), "coef", None, None, None),
    )
    return jax.shard_map(
        per_device,
        mesh=mesh,
        in_specs=placed,
        out_specs=P(("parts", "track"), None),
        check_vma=False,
    )
```

```python
import functools

import jax
import jax.numpy as jnp
from jax import lax
from jax.experimental import pallas as pl
from jax.experimental.pallas import tpu as pltpu
from jax.sharding import PartitionSpec as P

HUBER = 2.0
F32 = jnp.float32
BF16 = jnp.bfloat16
NT = (((1,), (1,)), ((), ()))
NN = (((1,), (0,)), ((), ()))


def dot(a, b, dims=NN):
    return lax.dot_general(a, b, dims, preferred_element_type=F32)


def iota(shape, dim):
    return lax.broadcasted_iota(jnp.int32, shape, dim)


def wrap(value, size):
    return lax.rem(value, size)


def kernel(
    dims, count_hbm, sid_hbm, obs_hbm, wts_hbm, coef_hbm, tile_hbm, sens_hbm, out_ref,
    count_ref, sid_ref, obs_ref, wts_ref, coef_ref, tile_ref,
    sens, asks, asked, answers, answered, outgoing, rows, preds, gsend, grecv,
    small_sem, sens_sem, ask_send, ask_recv, answer_send, answer_recv,
    row_send, row_recv, pred_send, pred_recv, grad_send, grad_recv,
):
    nt, nm, nc, ns, hk, lr, nh = dims
    owners, total = nt * nm, nt * nm * nc
    slots = 128
    per = coef_ref.shape[0]
    nq = sid_ref.shape[0]
    entries = ns * hk
    wide = nt * lr
    t, m, c = lax.axis_index("track"), lax.axis_index("tm"), lax.axis_index("coef")
    own = t * nm + m
    me = own * nc + c
    mesh_ids = pl.DeviceIdType.MESH

    def each(act, tms, coefs):
        @pl.loop(1, nt)
        def _(dt):
            for dm in range(tms):
                for dc in range(coefs):
                    act(dt, dm, dc)

        for dm in range(tms):
            for dc in range(coefs):
                if dm or dc:
                    act(0, dm, dc)

    def peer(dt, dm, dc):
        return wrap(t + dt, nt), wrap(m + dm, nm), wrap(c + dc, nc)

    def device(at):
        return {"track": at[0], "tm": at[1], "coef": at[2]}

    pairs = (
        (tile_hbm, tile_ref), (count_hbm, count_ref), (sid_hbm, sid_ref), (obs_hbm, obs_ref),
        (wts_hbm, wts_ref), (coef_hbm, coef_ref),
    )
    small = [
        pltpu.make_async_copy(source, target, small_sem.at[i])
        for i, (source, target) in enumerate(pairs)
    ]
    for load in small:
        load.start()
    barrier = pltpu.get_barrier_semaphore()

    def greet(dt, dm, dc):
        pl.semaphore_signal(
            barrier, inc=1, device_id=device(peer(dt, dm, dc)), device_id_type=mesh_ids
        )

    each(greet, nm, nc)
    sector_rows = hk * 3 * slots
    loads = [
        pltpu.make_async_copy(
            sens_hbm.at[pl.ds(s * sector_rows, sector_rows)],
            sens.at[pl.ds(s * sector_rows, sector_rows)],
            sens_sem.at[s],
        )
        for s in range(ns)
    ]
    for load in loads:
        load.start()

    def ask_copy(dt, source):
        at = peer(dt, 0, 0)
        return pltpu.make_async_remote_copy(
            src_ref=asks.at[at[0]], dst_ref=asked.at[source],
            send_sem=ask_send.at[dt], recv_sem=ask_recv.at[source],
            device_id=device(at), device_id_type=mesh_ids,
        )

    def answer_copy(dt, source):
        at = peer(dt, 0, 0)
        return pltpu.make_async_remote_copy(
            src_ref=answers.at[pl.ds(pl.multiple_of(at[0] * lr, lr), lr)],
            dst_ref=answered.at[pl.ds(pl.multiple_of(source * lr, lr), lr)],
            send_sem=answer_send.at[dt], recv_sem=answer_recv.at[source],
            device_id=device(at), device_id_type=mesh_ids,
        )

    def row_copy(dt, dm, source):
        at = peer(dt, dm, 0)
        return pltpu.make_async_remote_copy(
            src_ref=outgoing.at[at[0] * nm + at[1]], dst_ref=rows.at[source],
            send_sem=row_send.at[dt * nm + dm], recv_sem=row_recv.at[source],
            device_id=device(at), device_id_type=mesh_ids,
        )

    def pred_copy(dc, source):
        return pltpu.make_async_remote_copy(
            src_ref=preds.at[c], dst_ref=preds.at[source],
            send_sem=pred_send.at[dc], recv_sem=pred_recv.at[source],
            device_id=device(peer(0, 0, dc)), device_id_type=mesh_ids,
        )

    def grad_copy(dt, dm, dc, source):
        at = peer(dt, dm, dc)
        return pltpu.make_async_remote_copy(
            src_ref=gsend.at[pl.ds(pl.multiple_of(at[0] * lr, lr), lr)], dst_ref=grecv.at[source],
            send_sem=grad_send.at[(dt * nm + dm) * nc + dc], recv_sem=grad_recv.at[source],
            device_id=device(at), device_id_type=mesh_ids,
        )

    small[0].wait()
    small[1].wait()
    index = jnp.concatenate([tile_ref[:, pl.ds(k, 1)] for k in range(hk)], axis=0)
    sub = iota((ns, 1), 0)
    count = jnp.zeros((ns, 1), jnp.int32)
    for s in range(ns):
        count = jnp.where(sub == s, count_ref[s], count)
    active = jnp.concatenate(
        [jnp.where(c * hk + k < count, 1.0, 0.0) for k in range(hk)], axis=0
    )
    lane = iota((entries, 128), 1)
    named = (index >= lane * per) & (index < (lane + 1) * per)
    named_f = jnp.where(named, 1.0, 0.0)
    before = jnp.where(iota((entries, entries), 1) < iota((entries, entries), 0), 1.0, 0.0)
    rank = jnp.sum(dot(before.astype(BF16), named_f.astype(BF16)) * named_f, axis=1, keepdims=True)
    track = jnp.sum(jnp.where(named, lane, 0).astype(F32), axis=1, keepdims=True)
    within = index.astype(F32) - track * per + 1.0
    across = iota((entries, wide), 1).astype(F32)
    mine = (t * lr).astype(F32)
    for u in range(nt):
        asks[u] = jnp.sum(
            jnp.where((track == u) & (rank + mine == across), within, 0.0), axis=0, keepdims=True
        )
    lane_f = lane.astype(F32)
    shift = (lax.rem(me, 128 // lr) * lr).astype(F32)
    marks = []
    for u in range(nt):
        marks.append(
            jnp.sum(
                jnp.where((track == u) & (rank + shift == lane_f), within, 0.0), axis=0, keepdims=True
            )
        )
    spread = jnp.where(track * lr + rank == across, 1.0, 0.0)
    squeeze = spread.T.astype(BF16)
    pick = jnp.where(active > 0.5, spread, 0.0).astype(BF16)
    asked[t] = asks[t]
    pl.semaphore_wait(barrier, total - 1)

    @pl.loop(1, nt)
    def _(dt):
        ask_copy(dt, t).start()

    for load in small[2:5]:
        load.wait()
    ri, rj = iota((128, 256), 0), iota((128, 256), 1)
    tri = jnp.where((ri < rj) | (rj >= 128), 1.0, 0.0).astype(BF16)
    slot_at = iota((slots, 128), 0).astype(F32)
    owner_at = iota((owners, 128), 0) * ns
    first = owner_at.astype(F32)
    key_at = iota((owners * nh, 128), 0).astype(F32)
    ids = [sid_ref[pl.ds(q, 1), :].astype(F32) for q in range(nq)]
    belongs = [jnp.where((i >= first) & (i < first + ns), 1.0, 0.0) for i in ids]
    ahead = dot(jnp.concatenate(belongs, axis=0).astype(BF16), tri)
    base = jnp.zeros((owners, 128), F32)
    high, low, put = [], [], []
    for q in range(nq):
        hit = belongs[q]
        order = ahead[q * owners:(q + 1) * owners, :128] + base
        base = base + ahead[q * owners:(q + 1) * owners, 128:]
        order = jnp.sum(hit * order, axis=0, keepdims=True)
        to = jnp.sum(hit * first, axis=0, keepdims=True)
        half = jnp.zeros_like(order)
        for h in range(1, nh):
            half = half + jnp.where(order >= h * 128.0, 1.0, 0.0)
        key = to * (nh / ns) + half
        put.append(jnp.where(order - half * 128.0 == slot_at, 1.0, 0.0).astype(BF16))
        lanes = pl.ds(q * 128, 128)
        piece = jnp.concatenate(
            [obs_ref[:, lanes], wts_ref[:, lanes], ids[q] - to + 1.0, jnp.zeros((1, 128), F32)], axis=0
        )
        upper = piece.astype(BF16).astype(F32)
        lower = piece - upper
        chosen = jnp.where(key == key_at, 1.0, 0.0)
        high.append(
            jnp.concatenate([chosen[i:i + 1] * upper for i in range(owners * nh)], axis=0).astype(BF16)
        )
        low.append(
            jnp.concatenate([chosen[i:i + 1] * lower for i in range(owners * nh)], axis=0).astype(BF16)
        )
    put = jnp.concatenate(put, axis=1)
    sorted_rows = dot(jnp.concatenate(high, axis=1), put, NT)
    sorted_rows = sorted_rows + dot(jnp.concatenate(low, axis=1), put, NT)
    outgoing[...] = sorted_rows.reshape(owners, nh * 8, 128)
    rows[own] = outgoing[own]

    @pl.loop(1, nt)
    def _(dt):
        ask_copy(0, wrap(t + dt, nt)).wait_recv()

    small[5].wait()
    wanted = asked[0]
    for u in range(1, nt):
        wanted = wanted + asked[u]
    wanted = jnp.broadcast_to(wanted, (128, wide)).T
    per_lane = iota((wide, 128), 1).astype(F32) + 1.0
    chosen = jnp.concatenate(
        [
            jnp.where(wanted == per_lane + (i * 128.0), 1.0, 0.0).astype(BF16)
            for i in range((per + 127) // 128)
        ],
        axis=1,
    )
    if per % 128:
        chosen = chosen[:, :per]
    answers[...] = dot(chosen, coef_ref[...].astype(BF16)).astype(BF16)

    @pl.loop(1, nt)
    def _(dt):
        answer_copy(dt, t).start()

    def send_rows(dt, dm, dc):
        row_copy(dt, dm, own).start()

    each(send_rows, nm, 1)
    own_answer = pl.ds(pl.multiple_of(t * lr, lr), lr)
    answered[own_answer] = answers[own_answer]

    @pl.loop(1, nt)
    def _(dt):
        answer_copy(0, wrap(t + dt, nt)).wait_recv()

    blocks = dot(pick, answered[...])
    wide_blocks = jnp.concatenate(
        [blocks[k * ns:(k + 1) * ns] for k in range(hk)], axis=1
    ).astype(BF16)
    pixels = 3 * slots

    def tile(s, k):
        return sens[pl.ds((s * hk + k) * pixels, pixels), :]

    which = iota((ns, pixels), 0)
    pred = jnp.zeros((ns, pixels), F32)
    for s in range(ns):
        loads[s].wait()
        part = dot(wide_blocks, jnp.concatenate([tile(s, k) for k in range(hk)], axis=1), NT)
        pred = jnp.where(which == s, part, pred)
    preds[c] = pred

    @pl.loop(1, nc)
    def _(dc):
        pred_copy(dc, c).start()

    def take_rows(dt, dm, dc):
        at = peer(dt, dm, 0)
        row_copy(0, 0, at[0] * nm + at[1]).wait_recv()

    each(take_rows, nm, 1)

    sector = iota((ns, 128), 0).astype(F32) + 1.0
    group = min(owners, 8)

    def source_rows(step, carry):
        base, grid = carry
        got = [rows[step * group + j] for j in range(group)]
        pieces = [part[q * 8:(q + 1) * 8] for part in got for q in range(nh)]
        hits = [jnp.where(piece[6:7] == sector, 1.0, 0.0) for piece in pieces]
        ahead = dot(jnp.concatenate(hits, axis=0).astype(BF16), tri)
        put, high, low = [], [], []
        for q, (hit, piece) in enumerate(zip(hits, pieces)):
            rank_q = ahead[q * ns:(q + 1) * ns, :128] + base
            base = base + ahead[q * ns:(q + 1) * ns, 128:]
            slot = jnp.sum(hit * rank_q, axis=0, keepdims=True)
            put.append(jnp.where(slot == slot_at, 1.0, 0.0).astype(BF16))
            chunk = jnp.concatenate([hit * piece[i:i + 1] for i in range(6)], axis=0)
            upper = chunk.astype(BF16)
            high.append(upper)
            low.append((chunk - upper.astype(F32)).astype(BF16))
        both = jnp.concatenate(
            [jnp.concatenate(high, axis=1), jnp.concatenate(low, axis=1)], axis=0
        )
        return base, grid + dot(both, jnp.concatenate(put, axis=1), NT)

    carry = (jnp.zeros((ns, 128), F32), jnp.zeros((12 * ns, slots), F32))
    if owners == group:
        _, grid = source_rows(0, carry)
    else:
        _, grid = lax.fori_loop(0, owners // group, source_rows, carry)
    grid = grid[:6 * ns] + grid[6 * ns:]

    @pl.loop(1, nc)
    def _(dc):
        pred_copy(0, wrap(c + dc, nc)).wait_recv()

    pred = preds[0]
    for i in range(1, nc):
        pred = pred + preds[i]
    forces = []
    for i in range(3):
        w = grid[(3 + i) * ns:(4 + i) * ns]
        scaled = w * (pred[:, i * slots:(i + 1) * slots] - grid[i * ns:(i + 1) * ns])
        forces.append(w * scaled * lax.rsqrt(1.0 + (scaled / HUBER) ** 2))
    force = jnp.concatenate(forces, axis=1).astype(BF16)
    which = iota((ns, hk * 128), 0)
    grad = jnp.zeros((ns, hk * 128), F32)
    for s in range(ns):
        part = dot(force, jnp.concatenate([tile(s, k) for k in range(hk)], axis=1))
        grad = jnp.where(which == s, part, grad)
    grad = jnp.concatenate([grad[:, k * 128:(k + 1) * 128] for k in range(hk)], axis=0)
    grad = jnp.where(active > 0.5, grad, 0.0).astype(BF16)
    packed = dot(squeeze, grad)
    line = iota((nt * lr, 128), 0)
    for u in range(nt):
        packed = jnp.where(line == u * lr + lr - 1, marks[u], packed)
    gsend[...] = packed.astype(BF16)
    grecv[me] = gsend[pl.ds(pl.multiple_of(t * lr, lr), lr)]

    def send_grads(dt, dm, dc):
        grad_copy(dt, dm, dc, me).start()

    each(send_grads, nm, nc)

    def take_grads(dt, dm, dc):
        at = peer(dt, dm, dc)
        grad_copy(0, 0, 0, (at[0] * nm + at[1]) * nc + at[2]).wait_recv()

    each(take_grads, nm, nc)

    together = 128 // lr
    at = iota((per, 128), 0).astype(F32) + 1.0

    def gather_group(g, acc):
        base = g * together
        mark = jnp.zeros((1, 128), F32)
        for i in range(together):
            mark = mark + grecv[base + i].astype(F32)[lr - 1:lr]
        terms = jnp.concatenate([grecv[base + i] for i in range(together)], axis=0)
        return acc + dot(jnp.where(at == mark, 1.0, 0.0).astype(BF16), terms)

    out_ref[...] = lax.fori_loop(0, total // together, gather_group, jnp.zeros((per, 128), F32))

    @pl.loop(1, nt)
    def _(dt):
        ask_copy(dt, t).wait_send()
        answer_copy(dt, t).wait_send()

    def sent_rows(dt, dm, dc):
        row_copy(dt, dm, own).wait_send()

    each(sent_rows, nm, 1)

    @pl.loop(1, nc)
    def _(dc):
        pred_copy(dc, c).wait_send()

    def sent_grads(dt, dm, dc):
        grad_copy(dt, dm, dc, me).wait_send()

    each(sent_grads, nm, nc)


def per_device(sector_ids, observed, weights, coefficients, tile_index, tile_count, sensitivity):
    nt, nm, nc = lax.axis_size("track"), lax.axis_size("tm"), lax.axis_size("coef")
    ns, hk = tile_index.shape
    per, width = coefficients.shape
    nq = sector_ids.shape[0] // 128
    slots = sensitivity.shape[3]
    owners, total = nt * nm, nt * nm * nc
    cap = 2 * ns * hk // nt
    lr = (cap + 1 + 15) // 16 * 16
    nh = (2 * sector_ids.shape[0] // owners + 127) // 128
    flat = ns * hk * 3 * slots
    vmem = pl.BlockSpec(memory_space=pltpu.VMEM)
    dma = pltpu.SemaphoreType.DMA
    return pl.pallas_call(
        functools.partial(kernel, (nt, nm, nc, ns, hk, lr, nh)),
        out_shape=jax.ShapeDtypeStruct((per, width), F32),
        in_specs=[pl.BlockSpec(memory_space=pltpu.HBM)] * 7,
        out_specs=vmem,
        scratch_shapes=[
            pltpu.SMEM(tile_count.shape, jnp.int32),
            pltpu.VMEM((nq, 128), jnp.int32),
            pltpu.VMEM(observed.shape, F32),
            pltpu.VMEM(weights.shape, F32),
            pltpu.VMEM((per, width), F32),
            pltpu.VMEM(tile_index.shape, jnp.int32),
            pltpu.VMEM((flat, width), BF16),
            pltpu.VMEM((nt, 1, nt * lr), F32),
            pltpu.VMEM((nt, 1, nt * lr), F32),
            pltpu.VMEM((nt * lr, width), BF16),
            pltpu.VMEM((nt * lr, width), BF16),
            pltpu.VMEM((owners, nh * 8, 128), F32),
            pltpu.VMEM((owners, nh * 8, 128), F32),
            pltpu.VMEM((nc, ns, 3 * slots), F32),
            pltpu.VMEM((nt * lr, width), BF16),
            pltpu.VMEM((total, lr, width), BF16),
            dma((6,)), dma((ns,)),
            dma((nt,)), dma((nt,)),
            dma((nt,)), dma((nt,)),
            dma((owners,)), dma((owners,)),
            dma((nc,)), dma((nc,)),
            dma((total,)), dma((total,)),
        ],
        compiler_params=pltpu.CompilerParams(
            collective_id=0, has_side_effects=True, vmem_limit_bytes=64 * 1024 * 1024
        ),
    )(
        tile_count,
        sector_ids.reshape(nq, 128),
        observed,
        weights,
        coefficients,
        tile_index,
        sensitivity.reshape(flat, width),
    )


def solution(mesh):
    placed = (
        P(("parts", "track", "tm")),
        P(None, ("parts", "track", "tm")),
        P(None, ("parts", "track", "tm")),
        P(("parts", "track"), None),
        P(("parts", "track", "tm"), "coef"),
        P(("parts", "track", "tm")),
        P(("parts", "track", "tm"), "coef", None, None, None),
    )
    return jax.shard_map(
        per_device,
        mesh=mesh,
        in_specs=placed,
        out_specs=P(("parts", "track"), None),
        check_vma=False,
    )
```

```python
import functools

import jax
import jax.numpy as jnp
from jax import lax
from jax.experimental import pallas as pl
from jax.experimental.pallas import tpu as pltpu
from jax.sharding import PartitionSpec as P

HUBER = 2.0
F32 = jnp.float32
BF16 = jnp.bfloat16
NT = (((1,), (1,)), ((), ()))
NN = (((1,), (0,)), ((), ()))


def dot(a, b, dims=NN):
    return lax.dot_general(a, b, dims, preferred_element_type=F32)


def iota(shape, dim):
    return lax.broadcasted_iota(jnp.int32, shape, dim)


def wrap(value, size):
    return lax.rem(value, size)


def kernel(
    dims, count_hbm, sid_hbm, obs_hbm, wts_hbm, coef_hbm, tile_hbm, sens_hbm, out_ref,
    count_ref, sid_ref, obs_ref, wts_ref, coef_ref, tile_ref,
    sens, asks, asked, answers, answered, outgoing, rows, preds, gsend, grecv,
    small_sem, sens_sem, ask_send, ask_recv, answer_send, answer_recv,
    row_send, row_recv, pred_send, pred_recv, grad_send, grad_recv,
):
    nt, nm, nc, ns, hk, lr, nh = dims
    owners, total = nt * nm, nt * nm * nc
    slots = 128
    per = coef_ref.shape[0]
    nq = sid_ref.shape[0]
    entries = ns * hk
    wide = nt * lr
    t, m, c = lax.axis_index("track"), lax.axis_index("tm"), lax.axis_index("coef")
    own = t * nm + m
    me = own * nc + c
    mesh_ids = pl.DeviceIdType.MESH

    def each(act, tms, coefs):
        @pl.loop(1, nt)
        def _(dt):
            for dm in range(tms):
                for dc in range(coefs):
                    act(dt, dm, dc)

        for dm in range(tms):
            for dc in range(coefs):
                if dm or dc:
                    act(0, dm, dc)

    def peer(dt, dm, dc):
        return wrap(t + dt, nt), wrap(m + dm, nm), wrap(c + dc, nc)

    def device(at):
        return {"track": at[0], "tm": at[1], "coef": at[2]}

    pairs = (
        (tile_hbm, tile_ref), (count_hbm, count_ref), (sid_hbm, sid_ref), (obs_hbm, obs_ref),
        (wts_hbm, wts_ref), (coef_hbm, coef_ref),
    )
    small = [
        pltpu.make_async_copy(source, target, small_sem.at[i])
        for i, (source, target) in enumerate(pairs)
    ]
    for load in small:
        load.start()
    barrier = pltpu.get_barrier_semaphore()

    def greet(dt, dm, dc):
        pl.semaphore_signal(
            barrier, inc=1, device_id=device(peer(dt, dm, dc)), device_id_type=mesh_ids
        )

    each(greet, nm, nc)
    sector_rows = hk * 3 * slots
    loads = [
        pltpu.make_async_copy(
            sens_hbm.at[pl.ds(s * sector_rows, sector_rows)],
            sens.at[pl.ds(s * sector_rows, sector_rows)],
            sens_sem.at[s],
        )
        for s in range(ns)
    ]
    for load in loads:
        load.start()

    def ask_copy(dt, source):
        at = peer(dt, 0, 0)
        return pltpu.make_async_remote_copy(
            src_ref=asks.at[at[0]], dst_ref=asked.at[source],
            send_sem=ask_send.at[dt], recv_sem=ask_recv.at[source],
            device_id=device(at), device_id_type=mesh_ids,
        )

    def answer_copy(dt, source):
        at = peer(dt, 0, 0)
        return pltpu.make_async_remote_copy(
            src_ref=answers.at[pl.ds(pl.multiple_of(at[0] * lr, lr), lr)],
            dst_ref=answered.at[pl.ds(pl.multiple_of(source * lr, lr), lr)],
            send_sem=answer_send.at[dt], recv_sem=answer_recv.at[source],
            device_id=device(at), device_id_type=mesh_ids,
        )

    def row_copy(dt, dm, source):
        at = peer(dt, dm, 0)
        return pltpu.make_async_remote_copy(
            src_ref=outgoing.at[at[0] * nm + at[1]], dst_ref=rows.at[source],
            send_sem=row_send.at[dt * nm + dm], recv_sem=row_recv.at[source],
            device_id=device(at), device_id_type=mesh_ids,
        )

    def pred_copy(dc, source):
        return pltpu.make_async_remote_copy(
            src_ref=preds.at[c], dst_ref=preds.at[source],
            send_sem=pred_send.at[dc], recv_sem=pred_recv.at[source],
            device_id=device(peer(0, 0, dc)), device_id_type=mesh_ids,
        )

    def grad_copy(dt, dm, dc, source):
        at = peer(dt, dm, dc)
        return pltpu.make_async_remote_copy(
            src_ref=gsend.at[pl.ds(pl.multiple_of(at[0] * lr, lr), lr)], dst_ref=grecv.at[source],
            send_sem=grad_send.at[(dt * nm + dm) * nc + dc], recv_sem=grad_recv.at[source],
            device_id=device(at), device_id_type=mesh_ids,
        )

    small[0].wait()
    index = jnp.concatenate([tile_ref[:, pl.ds(k, 1)] for k in range(hk)], axis=0)
    lane = iota((entries, 128), 1)
    named = (index >= lane * per) & (index < (lane + 1) * per)
    named_f = jnp.where(named, 1.0, 0.0)
    before = jnp.where(iota((entries, entries), 1) < iota((entries, entries), 0), 1.0, 0.0)
    rank = jnp.sum(dot(before.astype(BF16), named_f.astype(BF16)) * named_f, axis=1, keepdims=True)
    track = jnp.sum(jnp.where(named, lane, 0).astype(F32), axis=1, keepdims=True)
    within = index.astype(F32) - track * per + 1.0
    across = iota((entries, wide), 1).astype(F32)
    mine = (t * lr).astype(F32)
    for u in range(nt):
        asks[u] = jnp.sum(
            jnp.where((track == u) & (rank + mine == across), within, 0.0), axis=0, keepdims=True
        )
    asked[t] = asks[t]
    pl.semaphore_wait(barrier, total - 1)

    @pl.loop(1, nt)
    def _(dt):
        ask_copy(dt, t).start()

    for load in small[2:5]:
        load.wait()
    ri, rj = iota((128, 256), 0), iota((128, 256), 1)
    tri = jnp.where((ri < rj) | (rj >= 128), 1.0, 0.0).astype(BF16)
    slot_at = iota((slots, 128), 0).astype(F32)
    owner_at = iota((owners, 128), 0) * ns
    first = owner_at.astype(F32)
    key_at = iota((owners * nh, 128), 0).astype(F32)
    ids = [sid_ref[pl.ds(q, 1), :].astype(F32) for q in range(nq)]
    belongs = [jnp.where((i >= first) & (i < first + ns), 1.0, 0.0) for i in ids]
    ahead = dot(jnp.concatenate(belongs, axis=0).astype(BF16), tri)
    base = jnp.zeros((owners, 128), F32)
    high, low, put = [], [], []
    for q in range(nq):
        hit = belongs[q]
        order = ahead[q * owners:(q + 1) * owners, :128] + base
        base = base + ahead[q * owners:(q + 1) * owners, 128:]
        order = jnp.sum(hit * order, axis=0, keepdims=True)
        to = jnp.sum(hit * first, axis=0, keepdims=True)
        half = jnp.zeros_like(order)
        for h in range(1, nh):
            half = half + jnp.where(order >= h * 128.0, 1.0, 0.0)
        key = to * (nh / ns) + half
        put.append(jnp.where(order - half * 128.0 == slot_at, 1.0, 0.0).astype(BF16))
        lanes = pl.ds(q * 128, 128)
        piece = jnp.concatenate(
            [obs_ref[:, lanes], wts_ref[:, lanes], ids[q] - to + 1.0, jnp.zeros((1, 128), F32)], axis=0
        )
        upper = piece.astype(BF16).astype(F32)
        lower = piece - upper
        chosen = jnp.where(key == key_at, 1.0, 0.0)
        high.append(
            jnp.concatenate([chosen[i:i + 1] * upper for i in range(owners * nh)], axis=0).astype(BF16)
        )
        low.append(
            jnp.concatenate([chosen[i:i + 1] * lower for i in range(owners * nh)], axis=0).astype(BF16)
        )
    put = jnp.concatenate(put, axis=1)
    sorted_rows = dot(jnp.concatenate(high, axis=1), put, NT)
    sorted_rows = sorted_rows + dot(jnp.concatenate(low, axis=1), put, NT)
    outgoing[...] = sorted_rows.reshape(owners, nh * 8, 128)
    rows[own] = outgoing[own]

    @pl.loop(1, nt)
    def _(dt):
        ask_copy(0, wrap(t + dt, nt)).wait_recv()

    small[5].wait()
    wanted = asked[0]
    for u in range(1, nt):
        wanted = wanted + asked[u]
    wanted = jnp.broadcast_to(wanted, (128, wide)).T
    per_lane = iota((wide, 128), 1).astype(F32) + 1.0
    chosen = jnp.concatenate(
        [
            jnp.where(wanted == per_lane + (i * 128.0), 1.0, 0.0).astype(BF16)
            for i in range((per + 127) // 128)
        ],
        axis=1,
    )
    if per % 128:
        chosen = chosen[:, :per]
    answers[...] = dot(chosen, coef_ref[...].astype(BF16)).astype(BF16)

    @pl.loop(1, nt)
    def _(dt):
        answer_copy(dt, t).start()

    def send_rows(dt, dm, dc):
        row_copy(dt, dm, own).start()

    each(send_rows, nm, 1)
    small[1].wait()
    sub = iota((ns, 1), 0)
    count = jnp.zeros((ns, 1), jnp.int32)
    for s in range(ns):
        count = jnp.where(sub == s, count_ref[s], count)
    active = jnp.concatenate(
        [jnp.where(c * hk + k < count, 1.0, 0.0) for k in range(hk)], axis=0
    )
    lane_f = lane.astype(F32)
    shift = (lax.rem(me, 128 // lr) * lr).astype(F32)
    marks = []
    for u in range(nt):
        marks.append(
            jnp.sum(
                jnp.where((track == u) & (rank + shift == lane_f), within, 0.0), axis=0, keepdims=True
            )
        )
    spread = jnp.where(track * lr + rank == across, 1.0, 0.0)
    squeeze = spread.T.astype(BF16)
    pick = jnp.where(active > 0.5, spread, 0.0).astype(BF16)
    own_answer = pl.ds(pl.multiple_of(t * lr, lr), lr)
    answered[own_answer] = answers[own_answer]

    @pl.loop(1, nt)
    def _(dt):
        answer_copy(0, wrap(t + dt, nt)).wait_recv()

    blocks = dot(pick, answered[...])
    ones = jnp.ones((ns, 256), BF16)
    pixels = 3 * slots

    def tile(s, k):
        return sens[pl.ds((s * hk + k) * pixels, pixels), :]

    which = iota((ns, pixels), 0)
    pred = jnp.zeros((ns, pixels), F32)
    for s in range(ns):
        loads[s].wait()
        terms = sum(
            tile(s, k).astype(F32) * blocks[k * ns + s:k * ns + s + 1] for k in range(hk)
        )
        upper = terms.astype(BF16)
        lower = (terms - upper.astype(F32)).astype(BF16)
        part = dot(ones, jnp.concatenate([upper, lower], axis=1), NT)
        pred = jnp.where(which == s, part, pred)
    preds[c] = pred

    @pl.loop(1, nc)
    def _(dc):
        pred_copy(dc, c).start()

    def take_rows(dt, dm, dc):
        at = peer(dt, dm, 0)
        row_copy(0, 0, at[0] * nm + at[1]).wait_recv()

    each(take_rows, nm, 1)

    sector = iota((ns, 128), 0).astype(F32) + 1.0
    group = min(owners, 8)

    def source_rows(step, carry):
        base, grid = carry
        got = [rows[step * group + j] for j in range(group)]
        pieces = [part[q * 8:(q + 1) * 8] for part in got for q in range(nh)]
        hits = [jnp.where(piece[6:7] == sector, 1.0, 0.0) for piece in pieces]
        ahead = dot(jnp.concatenate(hits, axis=0).astype(BF16), tri)
        put, high, low = [], [], []
        for q, (hit, piece) in enumerate(zip(hits, pieces)):
            rank_q = ahead[q * ns:(q + 1) * ns, :128] + base
            base = base + ahead[q * ns:(q + 1) * ns, 128:]
            slot = jnp.sum(hit * rank_q, axis=0, keepdims=True)
            put.append(jnp.where(slot == slot_at, 1.0, 0.0).astype(BF16))
            chunk = jnp.concatenate([hit * piece[i:i + 1] for i in range(6)], axis=0)
            upper = chunk.astype(BF16)
            high.append(upper)
            low.append((chunk - upper.astype(F32)).astype(BF16))
        both = jnp.concatenate(
            [jnp.concatenate(high, axis=1), jnp.concatenate(low, axis=1)], axis=0
        )
        return base, grid + dot(both, jnp.concatenate(put, axis=1), NT)

    carry = (jnp.zeros((ns, 128), F32), jnp.zeros((12 * ns, slots), F32))
    if owners == group:
        _, grid = source_rows(0, carry)
    else:
        _, grid = lax.fori_loop(0, owners // group, source_rows, carry)
    grid = grid[:6 * ns] + grid[6 * ns:]

    @pl.loop(1, nc)
    def _(dc):
        pred_copy(0, wrap(c + dc, nc)).wait_recv()

    pred = preds[0]
    for i in range(1, nc):
        pred = pred + preds[i]
    forces = []
    for i in range(3):
        w = grid[(3 + i) * ns:(4 + i) * ns]
        scaled = w * (pred[:, i * slots:(i + 1) * slots] - grid[i * ns:(i + 1) * ns])
        forces.append(w * scaled * lax.rsqrt(1.0 + (scaled / HUBER) ** 2))
    force = jnp.concatenate(forces, axis=1).astype(BF16)
    which = iota((ns, hk * 128), 0)
    grad = jnp.zeros((ns, hk * 128), F32)
    for s in range(ns):
        part = dot(force, jnp.concatenate([tile(s, k) for k in range(hk)], axis=1))
        grad = jnp.where(which == s, part, grad)
    grad = jnp.concatenate([grad[:, k * 128:(k + 1) * 128] for k in range(hk)], axis=0)
    grad = jnp.where(active > 0.5, grad, 0.0).astype(BF16)
    packed = dot(squeeze, grad)
    line = iota((nt * lr, 128), 0)
    for u in range(nt):
        packed = jnp.where(line == u * lr + lr - 1, marks[u], packed)
    gsend[...] = packed.astype(BF16)
    grecv[me] = gsend[pl.ds(pl.multiple_of(t * lr, lr), lr)]

    def send_grads(dt, dm, dc):
        grad_copy(dt, dm, dc, me).start()

    each(send_grads, nm, nc)

    def take_grads(dt, dm, dc):
        at = peer(dt, dm, dc)
        grad_copy(0, 0, 0, (at[0] * nm + at[1]) * nc + at[2]).wait_recv()

    each(take_grads, nm, nc)

    together = 128 // lr
    at = iota((per, 128), 0).astype(F32) + 1.0

    bundle = min(total // together, 4)

    def gather_groups(step, acc):
        finds, terms = [], []
        for g in range(bundle):
            base = (step * bundle + g) * together
            parts = [grecv[base + i] for i in range(together)]
            mark = sum(part.astype(F32)[lr - 1:lr] for part in parts)
            finds.append(jnp.where(at == mark, 1.0, 0.0).astype(BF16))
            terms.extend(parts)
        return acc + dot(jnp.concatenate(finds, axis=1), jnp.concatenate(terms, axis=0))

    acc = jnp.zeros((per, 128), F32)
    if total == bundle * together:
        out_ref[...] = gather_groups(0, acc)
    else:
        out_ref[...] = lax.fori_loop(0, total // (bundle * together), gather_groups, acc)

    @pl.loop(1, nt)
    def _(dt):
        ask_copy(dt, t).wait_send()
        answer_copy(dt, t).wait_send()

    def sent_rows(dt, dm, dc):
        row_copy(dt, dm, own).wait_send()

    each(sent_rows, nm, 1)

    @pl.loop(1, nc)
    def _(dc):
        pred_copy(dc, c).wait_send()

    def sent_grads(dt, dm, dc):
        grad_copy(dt, dm, dc, me).wait_send()

    each(sent_grads, nm, nc)


def per_device(sector_ids, observed, weights, coefficients, tile_index, tile_count, sensitivity):
    nt, nm, nc = lax.axis_size("track"), lax.axis_size("tm"), lax.axis_size("coef")
    ns, hk = tile_index.shape
    per, width = coefficients.shape
    nq = sector_ids.shape[0] // 128
    slots = sensitivity.shape[3]
    owners, total = nt * nm, nt * nm * nc
    cap = 2 * ns * hk // nt
    lr = (cap + 1 + 15) // 16 * 16
    nh = (2 * sector_ids.shape[0] // owners + 127) // 128
    flat = ns * hk * 3 * slots
    vmem = pl.BlockSpec(memory_space=pltpu.VMEM)
    dma = pltpu.SemaphoreType.DMA
    return pl.pallas_call(
        functools.partial(kernel, (nt, nm, nc, ns, hk, lr, nh)),
        out_shape=jax.ShapeDtypeStruct((per, width), F32),
        in_specs=[pl.BlockSpec(memory_space=pltpu.HBM)] * 7,
        out_specs=vmem,
        scratch_shapes=[
            pltpu.SMEM(tile_count.shape, jnp.int32),
            pltpu.VMEM((nq, 128), jnp.int32),
            pltpu.VMEM(observed.shape, F32),
            pltpu.VMEM(weights.shape, F32),
            pltpu.VMEM((per, width), F32),
            pltpu.VMEM(tile_index.shape, jnp.int32),
            pltpu.VMEM((flat, width), BF16),
            pltpu.VMEM((nt, 1, nt * lr), F32),
            pltpu.VMEM((nt, 1, nt * lr), F32),
            pltpu.VMEM((nt * lr, width), BF16),
            pltpu.VMEM((nt * lr, width), BF16),
            pltpu.VMEM((owners, nh * 8, 128), F32),
            pltpu.VMEM((owners, nh * 8, 128), F32),
            pltpu.VMEM((nc, ns, 3 * slots), F32),
            pltpu.VMEM((nt * lr, width), BF16),
            pltpu.VMEM((total, lr, width), BF16),
            dma((6,)), dma((ns,)),
            dma((nt,)), dma((nt,)),
            dma((nt,)), dma((nt,)),
            dma((owners,)), dma((owners,)),
            dma((nc,)), dma((nc,)),
            dma((total,)), dma((total,)),
        ],
        compiler_params=pltpu.CompilerParams(
            collective_id=0, has_side_effects=True, vmem_limit_bytes=64 * 1024 * 1024
        ),
    )(
        tile_count,
        sector_ids.reshape(nq, 128),
        observed,
        weights,
        coefficients,
        tile_index,
        sensitivity.reshape(flat, width),
    )


def solution(mesh):
    placed = (
        P(("parts", "track", "tm")),
        P(None, ("parts", "track", "tm")),
        P(None, ("parts", "track", "tm")),
        P(("parts", "track"), None),
        P(("parts", "track", "tm"), "coef"),
        P(("parts", "track", "tm")),
        P(("parts", "track", "tm"), "coef", None, None, None),
    )
    return jax.shard_map(
        per_device,
        mesh=mesh,
        in_specs=placed,
        out_specs=P(("parts", "track"), None),
        check_vma=False,
    )
```
